32 devices in a mesh: val: 4 (over y, core), cond: 8 (over z, x).
Axes of the slice: x: 2, y: 2, z: 4, core: 2. Of those that a mesh axis runs over, the one named last changes fastest.
Arguments:
- orb_val: bfloat16 [2, 4, 262144], P(None, 'val'), may hold values from -6 to 6
- orb_cond: bfloat16 [2, 8, 262144], P(None, 'cond'), may hold values from -6 to 6
- energies: float32 [4, 8], replicated, may hold values from 0.2 to 2
- gvec_map: int32 [8192], replicated, may hold values from 0 to 262143, as said below
Outputs:
- chi_zero: float32 [2, 8192, 8192], P(None, 'val', 'cond')
The draws below stay inside these ranges and needn't reach their ends.
Inputs may be any that keep to these rules, and one draw needn't show every extreme that they name: `gvec_map`: the 8192 entries are distinct grid cells, the 8192 cells nearest the anchor in signed frequencies (each index k read as k - 64 when k >= 32), ties on the sphere's surface broken at random, listed in random order; at the real sizes they lie within a sphere of radius about 12.5 grid units.
All inputs are finite; a program needn't handle non-finite values.
Results may differ from the reference program's by a relative error of at most 0.0048.
Values may be sent and summed in bfloat16 or wider, within the bound.
A program may use at most 64 MiB of HBM per device.

```python
import math
import jax
import jax.numpy as jnp
from jax import lax

NFFT = 64
NG = 8192
VB = 4
CB = 8


def draw_gvec_map(key, part):
    key = jax.random.fold_in(key, 7)
    tie_key = jax.random.fold_in(key, 1)
    order_key = jax.random.fold_in(key, 2)
    wave = jnp.arange(NFFT, dtype=jnp.int32)
    signed = jnp.where(wave >= NFFT // 2, wave - NFFT, wave)
    squares = signed * signed
    radius = (squares[:, None, None] + squares[None, :, None] + squares[None, None, :]).reshape(-1)
    ranks = jax.random.permutation(tie_key, NFFT ** 3).astype(jnp.int32)
    score = radius * NFFT ** 3 + ranks
    nearest = jnp.argsort(score, stable=True)[:NG].astype(jnp.int32)
    shuffle = jax.random.permutation(order_key, NG)
    return nearest[shuffle].astype(jnp.int32)


def shard_levels(key, dims, shards, low, high):
    factor_of = 1.0
    for axis_at, shards_of in shards:
        steps = jax.random.uniform(jax.random.fold_in(jax.random.fold_in(key, 6), axis_at), (shards_of,), jnp.float32, low / len(shards), high / len(shards))
        factor_of = factor_of * jnp.repeat(jnp.exp(steps), dims[axis_at] // shards_of).reshape((-1,) + (1,) * (len(dims) - 1 - axis_at))
    return factor_of


def scatter_about(stream_key, dims, width, most, pieces=(), kind=jnp.bfloat16):
    values = jax.random.normal(stream_key, dims, jnp.float32) * width
    if len(pieces) > 0:
        values = shard_levels(stream_key, dims, pieces, -0.22, 0.18) * values
    return jnp.clip(values, min=-most, max=most).astype(kind)


def setup_inputs(seed: int = 0) -> dict:
    keys = jax.random.split(jax.random.key(seed), 5)
    return {
        "orb_val": scatter_about(keys[0], (2, VB, NFFT ** 3), 1.0, 6.0, ((1, 4),)),
        "orb_cond": scatter_about(keys[1], (2, CB, NFFT ** 3), 1.0, 6.0, ((1, 8),)),
        "energies": jnp.clip(jnp.exp(jax.random.uniform(keys[2], (VB, CB), jnp.float32, math.log(0.2), math.log(2.0))), 0.2, 2.0),
        "gvec_map": draw_gvec_map(jax.random.fold_in(keys[4], 71), 0),
    }


def reference(orb_val, orb_cond, energies, gvec_map):
    side = NFFT
    cond_real = orb_cond[0].astype(jnp.float32)
    cond_imag = orb_cond[1].astype(jnp.float32)

    def one_band(bands):
        val_real = bands[0].astype(jnp.float32)[None, :]
        val_imag = bands[1].astype(jnp.float32)[None, :]
        pair_real = val_real * cond_real + val_imag * cond_imag
        pair_imag = val_real * cond_imag - val_imag * cond_real
        fields = lax.complex(pair_real, pair_imag).reshape(CB, side, side, side)
        spectrum = jnp.fft.fftn(fields, axes=(1, 2, 3)).reshape(CB, side * side * side)
        picked = spectrum[:, gvec_map]
        scale = float(side) ** -1.5
        return jnp.stack([jnp.real(picked) * scale, jnp.imag(picked) * scale])

    density = lax.map(one_band, (orb_val[0], orb_val[1]))
    density = jnp.transpose(density, (1, 0, 2, 3)).astype(jnp.bfloat16)
    weight = -2.0 / (float(VB * CB) * energies)
    weighted = (weight[None, :, :, None] * density.astype(jnp.float32)).astype(jnp.bfloat16)
    left = weighted.reshape(2 * VB * CB, NG).astype(jnp.float32)
    right = density.reshape(2 * VB * CB, NG).astype(jnp.float32)
    turned = jnp.concatenate([-density[1:2], density[0:1]], axis=0).reshape(2 * VB * CB, NG).astype(jnp.float32)
    real_part = jnp.einsum('pg,ph->gh', left, right)
    imag_part = jnp.einsum('pg,ph->gh', left, turned)
    return jnp.stack([real_part, imag_part])
```

```python
import functools
import math

import jax
import jax.numpy as jnp
import ml_dtypes
import numpy as np
from jax import lax
from jax.experimental import pallas as pl
from jax.experimental.pallas import tpu as pltpu
from jax.sharding import PartitionSpec as P

SIDE = 64
PAD = 32
F32 = jnp.float32
BF16 = jnp.bfloat16


def reach_of(side, count_g):
    wave = np.arange(side)
    signed = np.where(wave >= side // 2, wave - side, wave)
    squares = signed * signed
    radius = (squares[:, None, None] + squares[None, :, None] + squares[None, None, :]).reshape(-1)
    return math.isqrt(int(np.sort(radius)[count_g - 1]))


def split_high_low(matrix, axis):
    high = matrix.astype(ml_dtypes.bfloat16)
    low = (matrix - high.astype(np.float64)).astype(ml_dtypes.bfloat16)
    return np.concatenate([high, high, low], axis=axis)


def dft_matrices(reach):
    width = 2 * reach + 1
    waves = np.arange(width) - reach
    angle = 2.0 * np.pi * ((waves[None, :] * np.arange(SIDE)[:, None]) % SIDE) / SIDE
    cosine = np.zeros((SIDE, PAD))
    sine = np.zeros((SIDE, PAD))
    cosine[:, :width] = np.cos(angle)
    sine[:, :width] = np.sin(angle)
    full = np.zeros((2, SIDE, 2, PAD))
    full[0, :, 0] = cosine
    full[1, :, 0] = sine
    full[0, :, 1] = -sine
    full[1, :, 1] = cosine
    along_z = np.zeros((2, 2, SIDE, 2, 2, PAD))
    for low in range(2):
        along_z[:, low, :, :, low, :] = full
    along_z = along_z.reshape(4 * SIDE, 4 * PAD)
    along_y = full.reshape(2, SIDE // 2, 2, 2, PAD).transpose(3, 4, 0, 2, 1).reshape(2 * PAD, 2 * SIDE)
    along_x = full.transpose(2, 3, 0, 1).reshape(2 * PAD, 2 * SIDE) * float(SIDE) ** -1.5
    return split_high_low(along_z, 0), split_high_low(along_y, 1), split_high_low(along_x, 1)


def high_low(value):
    high = value.astype(BF16)
    return high, (value - high.astype(F32)).astype(BF16)


def regroup(parts, lane):
    results = []
    for j in range(4):
        total = None
        for i, part in enumerate(parts):
            shift = (32 * (i - j)) % 128
            moved = pltpu.roll(part, shift, 1) if shift else part
            total = moved if total is None else jnp.where(lane == i, moved, total)
        results.append(total)
    return results


def cube_of(val_ref, cond_ref, along_z, along_y, along_x, val_wide, cond_wide, by_z, by_y, quads):
    half = SIDE // 2
    val_wide[...] = val_ref[...].astype(F32)
    cond_wide[...] = cond_ref[...].astype(F32)
    quarter = SIDE // 4
    for x_high in range(quarter):
        rows = 4 * half
        real_rows = pl.ds(2 * rows * x_high, rows, stride=2)
        imag_rows = pl.ds(2 * rows * x_high + 1, rows, stride=2)
        val_real, val_imag = val_wide[real_rows, :], val_wide[imag_rows, :]
        cond_real, cond_imag = cond_wide[real_rows, :], cond_wide[imag_rows, :]
        real_high, real_low = high_low(val_real * cond_real + val_imag * cond_imag)
        imag_high, imag_low = high_low(val_real * cond_imag - val_imag * cond_real)
        for x_low in range(4):
            here = slice(half * x_low, half * (x_low + 1))
            there = slice(half * x_high, half * (x_high + 1))
            pieces = (real_high, imag_high, real_low, imag_low, real_high, imag_high)
            for at, piece in enumerate(pieces):
                by_z[x_low, there, 128 * at : 128 * (at + 1)] = piece[here]
    lane = lax.broadcasted_iota(jnp.int32, (1, 128), 1) // 32
    step = 128
    for start in range(0, quarter * half, step):
        parts = [
            jnp.dot(by_z[x_low, start : start + step, :], along_z[...], preferred_element_type=F32)
            for x_low in range(4)
        ]
        grouped = regroup(parts, lane)
        for inner in range(step // half):
            block = jnp.concatenate([g[half * inner : half * (inner + 1)] for g in grouped], axis=0)
            high, low = high_low(block)
            stacked = jnp.concatenate([high, low, high], axis=0)
            turned = jnp.dot(along_y[...], stacked, preferred_element_type=F32)
            x_high = start // half + inner
            by_y[128 * x_high : 128 * (x_high + 1), :] = jnp.concatenate([turned, turned], axis=0).T
    cubes = []
    for quad in range(quads):
        blocks = [by_y[pl.ds(4 * quad + i, SIDE, stride=PAD), :] for i in range(4)]
        real, imag = regroup(blocks, lane)[:2]
        high, low = high_low(jnp.concatenate([real, imag], axis=0))
        stacked = jnp.concatenate([high, low, high], axis=0)
        cubes.append(jnp.dot(along_x[...], stacked, preferred_element_type=F32).astype(BF16))
    return jnp.concatenate(cubes, axis=1)


def pick(cube, cells, reach):
    count = cells.shape[1]
    x_pos = ((cells >> 12) + reach) & (SIDE - 1)
    y_pos = ((cells >> 6) + reach) & (SIDE - 1)
    z_pos = (cells + reach) & (SIDE - 1)
    place = z_pos * PAD + y_pos
    rows = lax.broadcasted_iota(jnp.int32, (cube.shape[1], count), 0)
    chosen = jnp.where(rows == place, 1.0, 0.0).astype(BF16)
    lines = jnp.dot(cube, chosen, preferred_element_type=F32)
    plane = lax.broadcasted_iota(jnp.int32, (PAD, count), 0) == x_pos
    real = jnp.sum(jnp.where(plane, lines[:PAD], 0.0), axis=0, keepdims=True)
    imag = jnp.sum(jnp.where(plane, lines[PAD:], 0.0), axis=0, keepdims=True)
    return real, imag


def density_kernel(reach, val_ref, cond_ref, gvec_ref, wz_ref, wy_ref, wx_ref, out_ref, *scratch):
    quads = (2 * reach + 1 + 3) // 4
    cube_ref = scratch[-1]
    cube_ref[...] = cube_of(val_ref, cond_ref, wz_ref, wy_ref, wx_ref, *scratch[:-1], quads)
    step = 512

    @pl.loop(0, out_ref.shape[1] // step)
    def _(at):
        here = pl.ds(pl.multiple_of(at * step, step), step)
        real, imag = pick(cube_ref[...], gvec_ref[:, here], reach)
        out_ref[0:1, here] = real
        out_ref[1:2, here] = imag


def flat_rows(orbital):
    return orbital.reshape(2, -1, 128).transpose(1, 0, 2).reshape(-1, 128)


def on_device(orb_val, orb_cond, energies, gvec_map):
    count_g = gvec_map.shape[0]
    reach = reach_of(SIDE, count_g)
    along_z, along_y, along_x = dft_matrices(reach)
    rows = 2 * SIDE**3 // 128
    quads = (2 * reach + 1 + 3) // 4
    dense = pl.pallas_call(
        functools.partial(density_kernel, reach),
        out_shape=jax.ShapeDtypeStruct((2, count_g), F32),
        in_specs=[pl.BlockSpec(memory_space=pltpu.VMEM)] * 6,
        out_specs=pl.BlockSpec(memory_space=pltpu.VMEM),
        scratch_shapes=[
            pltpu.VMEM((rows, 128), F32),
            pltpu.VMEM((rows, 128), F32),
            pltpu.VMEM((4, SIDE // 4 * SIDE // 2, 6 * 128), BF16),
            pltpu.VMEM((SIDE * PAD, 128), F32),
            pltpu.VMEM((2 * PAD, 128 * quads), BF16),
        ],
        compiler_params=pltpu.CompilerParams(vmem_limit_bytes=48 * 2**20),
        name="density",
    )(
        flat_rows(orb_val),
        flat_rows(orb_cond),
        gvec_map.reshape(1, count_g),
        jnp.asarray(along_z),
        jnp.asarray(along_y),
        jnp.asarray(along_x),
    )
    total_val, total_cond = energies.shape
    val_pos = lax.axis_index("val")
    cond_pos = lax.axis_index("cond")
    density = dense[:, None, None, :].astype(BF16)
    weight_all = -2.0 / (float(total_val * total_cond) * energies)
    weight_local = lax.dynamic_slice(weight_all, (val_pos, cond_pos), (1, 1))
    weighted = (weight_local[None, :, :, None] * density.astype(F32)).astype(BF16)
    rows = lax.all_to_all(weighted, "val", split_axis=3, concat_axis=1, tiled=True)
    col_part = lax.all_to_all(density, "cond", split_axis=3, concat_axis=2, tiled=True)
    cols = lax.all_gather(col_part, "val", axis=1, tiled=True)
    rows_all = lax.all_gather(rows, "cond", axis=2, tiled=True)
    left = rows_all.reshape(-1, rows_all.shape[3])
    right = cols.reshape(-1, cols.shape[3])
    turned = jnp.concatenate([-cols[1:2], cols[0:1]], axis=0).reshape(-1, cols.shape[3])
    dims = (((0,), (0,)), ((), ()))
    real_sum = lax.dot_general(left, right, dims, preferred_element_type=F32)
    imag_sum = lax.dot_general(left, turned, dims, preferred_element_type=F32)
    return jnp.stack([real_sum, imag_sum])


def solution(mesh):
    return jax.shard_map(
        on_device,
        mesh=mesh,
        in_specs=(P(None, "val", None), P(None, "cond", None), P(), P()),
        out_specs=P(None, "val", "cond"),
        check_vma=False,
    )
```

```python
import functools
import math

import jax
import jax.numpy as jnp
import ml_dtypes
import numpy as np
from jax import lax
from jax.experimental import pallas as pl
from jax.experimental.pallas import tpu as pltpu
from jax.sharding import PartitionSpec as P

SIDE = 64
PAD = 32
F32 = jnp.float32
BF16 = jnp.bfloat16
MESH = pl.DeviceIdType.MESH


def reach_of(side, count_g):
    wave = np.arange(side)
    signed = np.where(wave >= side // 2, wave - side, wave)
    squares = signed * signed
    radius = (squares[:, None, None] + squares[None, :, None] + squares[None, None, :]).reshape(-1)
    return math.isqrt(int(np.sort(radius)[count_g - 1]))


def split_high_low(matrix, axis):
    high = matrix.astype(ml_dtypes.bfloat16)
    low = (matrix - high.astype(np.float64)).astype(ml_dtypes.bfloat16)
    return np.concatenate([high, high, low], axis=axis)


def dft_matrices(reach):
    width = 2 * reach + 1
    waves = np.arange(width) - reach
    angle = 2.0 * np.pi * ((waves[None, :] * np.arange(SIDE)[:, None]) % SIDE) / SIDE
    cosine = np.zeros((SIDE, PAD))
    sine = np.zeros((SIDE, PAD))
    cosine[:, :width] = np.cos(angle)
    sine[:, :width] = np.sin(angle)
    full = np.zeros((2, SIDE, 2, PAD))
    full[0, :, 0] = cosine
    full[1, :, 0] = sine
    full[0, :, 1] = -sine
    full[1, :, 1] = cosine
    along_z = np.zeros((2, 2, SIDE, 2, 2, PAD))
    for low in range(2):
        along_z[:, low, :, :, low, :] = full
    along_z = along_z.reshape(4 * SIDE, 4 * PAD)
    along_y = full.reshape(2, SIDE // 2, 2, 2, PAD).transpose(3, 4, 0, 2, 1).reshape(2 * PAD, 2 * SIDE)
    along_x = full.transpose(2, 3, 0, 1).reshape(2 * PAD, 2 * SIDE) * float(SIDE) ** -1.5
    return split_high_low(along_z, 0), split_high_low(along_y, 1), split_high_low(along_x, 1)


def high_low(value):
    high = value.astype(BF16)
    return high, (value - high.astype(F32)).astype(BF16)


def regroup(parts, lane):
    results = []
    for j in range(4):
        total = None
        for i, part in enumerate(parts):
            shift = (32 * (i - j)) % 128
            moved = pltpu.roll(part, shift, 1) if shift else part
            total = moved if total is None else jnp.where(lane == i, moved, total)
        results.append(total)
    return results


def cube_of(
    ready, weights_ready, val_ref, cond_ref, along_z, along_y, along_x, val_wide, cond_wide, by_z, by_y, quads
):
    half = SIDE // 2
    quarter = SIDE // 4
    for x_high in range(quarter):
        rows = 4 * half
        if x_high % 4 == 0:
            ready(x_high // 4)
        both = slice(2 * rows * x_high, 2 * rows * (x_high + 1))
        val_wide[both] = val_ref[both].astype(F32)
        cond_wide[both] = cond_ref[both].astype(F32)
        real_rows = pl.ds(2 * rows * x_high, rows, stride=2)
        imag_rows = pl.ds(2 * rows * x_high + 1, rows, stride=2)
        val_real, val_imag = val_wide[real_rows, :], val_wide[imag_rows, :]
        cond_real, cond_imag = cond_wide[real_rows, :], cond_wide[imag_rows, :]
        real_high, real_low = high_low(val_real * cond_real + val_imag * cond_imag)
        imag_high, imag_low = high_low(val_real * cond_imag - val_imag * cond_real)
        for x_low in range(4):
            here = slice(half * x_low, half * (x_low + 1))
            there = slice(half * x_high, half * (x_high + 1))
            pieces = (real_high, imag_high, real_low, imag_low, real_high, imag_high)
            for at, piece in enumerate(pieces):
                by_z[x_low, there, 128 * at : 128 * (at + 1)] = piece[here]
    weights_ready()
    lane = lax.broadcasted_iota(jnp.int32, (1, 128), 1) // 32
    step = 128
    for start in range(0, quarter * half, step):
        parts = [
            jnp.dot(by_z[x_low, start : start + step, :], along_z[...], preferred_element_type=F32)
            for x_low in range(4)
        ]
        grouped = regroup(parts, lane)
        for inner in range(step // half):
            block = jnp.concatenate([g[half * inner : half * (inner + 1)] for g in grouped], axis=0)
            high, low = high_low(block)
            stacked = jnp.concatenate([high, low, high], axis=0)
            turned = jnp.dot(along_y[...], stacked, preferred_element_type=F32)
            x_high = start // half + inner
            by_y[128 * x_high : 128 * (x_high + 1), :] = jnp.concatenate([turned, turned], axis=0).T
    cubes = []
    for quad in range(quads):
        blocks = [by_y[pl.ds(4 * quad + i, SIDE, stride=PAD), :] for i in range(4)]
        real, imag = regroup(blocks, lane)[:2]
        high, low = high_low(jnp.concatenate([real, imag], axis=0))
        stacked = jnp.concatenate([high, low, high], axis=0)
        cubes.append(jnp.dot(along_x[...], stacked, preferred_element_type=F32).astype(BF16))
    return jnp.concatenate(cubes, axis=1)


def pick(cube, cells, reach):
    count = cells.shape[1]
    x_pos = ((cells >> 12) + reach) & (SIDE - 1)
    y_pos = ((cells >> 6) + reach) & (SIDE - 1)
    z_pos = (cells + reach) & (SIDE - 1)
    place = z_pos * PAD + y_pos
    rows = lax.broadcasted_iota(jnp.int32, (cube.shape[1], count), 0)
    chosen = jnp.where(rows == place, 1.0, 0.0).astype(BF16)
    lines = jnp.dot(cube, chosen, preferred_element_type=F32)
    plane = lax.broadcasted_iota(jnp.int32, (PAD, count), 0) == x_pos
    real = jnp.sum(jnp.where(plane, lines[:PAD], 0.0), axis=0, keepdims=True)
    imag = jnp.sum(jnp.where(plane, lines[PAD:], 0.0), axis=0, keepdims=True)
    return real, imag


def density_kernel(
    reach,
    counts,
    val_ref,
    cond_ref,
    gvec_ref,
    energy_ref,
    wz_ref,
    wy_ref,
    wx_ref,
    rows_all,
    cols_all,
    val_in,
    cond_in,
    along_z,
    along_y,
    along_x,
    val_wide,
    cond_wide,
    by_z,
    by_y,
    cube_ref,
    row_stage,
    col_stage,
    row_send,
    col_send,
    in_sems,
    send_sems,
    recv_sems,
):
    n_val, n_cond = counts
    val_pos = lax.axis_index("val")
    cond_pos = lax.axis_index("cond")
    val_peers = [(lax.rem(val_pos + step, n_val), cond_pos) for step in range(1, n_val)]
    cond_peers = [(val_pos, lax.rem(cond_pos + step, n_cond)) for step in range(1, n_cond)]
    barrier = pltpu.get_barrier_semaphore()
    for peer in val_peers + cond_peers:
        pl.semaphore_signal(barrier, inc=1, device_id=peer, device_id_type=MESH)

    loads = [
        pltpu.make_async_copy(source, target, in_sems.at[at])
        for at, (source, target) in enumerate(
            ((wz_ref, along_z), (wy_ref, along_y), (wx_ref, along_x))
        )
    ]
    chunks = 4
    rows = val_in.shape[0] // chunks
    for chunk in range(chunks):
        here = slice(rows * chunk, rows * (chunk + 1))
        loads.append(pltpu.make_async_copy(val_ref.at[here], val_in.at[here], in_sems.at[3 + 2 * chunk]))
        loads.append(pltpu.make_async_copy(cond_ref.at[here], cond_in.at[here], in_sems.at[4 + 2 * chunk]))
    for load in loads[3:] + loads[:3]:
        load.start()

    def ready(chunk):
        loads[3 + 2 * chunk].wait()
        loads[4 + 2 * chunk].wait()

    def weights_ready():
        for load in loads[:3]:
            load.wait()

    quads = (2 * reach + 1 + 3) // 4
    cube_ref[...] = cube_of(
        ready, weights_ready, val_in, cond_in, along_z, along_y, along_x, val_wide, cond_wide, by_z, by_y, quads
    )
    step = 512
    row_lanes, col_lanes = rows_all.shape[3], cols_all.shape[3]
    count_g = gvec_ref.shape[1]
    row_segs = count_g // n_val // row_lanes
    col_segs = count_g // n_cond // col_lanes
    if row_segs < 8:
        row_stage[...] = jnp.zeros_like(row_stage)
    if col_segs < 8:
        col_stage[...] = jnp.zeros_like(col_stage)

    @pl.loop(0, count_g // step)
    def _(at):
        here = pl.ds(pl.multiple_of(at * step, step), step)
        picked = pick(cube_ref[...], gvec_ref[:, here], reach)
        for stage, lanes, segs in ((row_stage, row_lanes, row_segs), (col_stage, col_lanes, col_segs)):
            for piece in range(step // lanes):
                whole = at * (step // lanes) + piece
                for part in range(2):
                    stage[whole // segs, pl.ds(whole % segs + 8 * part, 1), :] = picked[part][
                        :, lanes * piece : lanes * (piece + 1)
                    ]

    total = float(energy_ref.shape[0] * energy_ref.shape[1])
    weights = -2.0 / (total * energy_ref[...])
    mine = (lax.broadcasted_iota(jnp.int32, weights.shape, 0) == val_pos) & (
        lax.broadcasted_iota(jnp.int32, weights.shape, 1) == cond_pos
    )
    weight = jnp.sum(jnp.where(mine, weights, 0.0))
    row_send[...] = (weight * row_stage[...].astype(BF16).astype(F32)).astype(BF16)
    col_send[...] = col_stage[...].astype(BF16)
    rows_all[cond_pos, val_pos] = row_send[val_pos]
    cols_all[cond_pos, val_pos] = col_send[cond_pos]

    def remote(source, target, at, peer):
        copy = pltpu.make_async_remote_copy(
            src_ref=source,
            dst_ref=target,
            send_sem=send_sems.at[at],
            recv_sem=recv_sems.at[at],
            device_id=peer,
            device_id_type=MESH,
        )
        copy.start()

    def wait_for(ref, sem):
        pltpu.make_async_copy(ref, ref, sem).wait()

    pl.semaphore_wait(barrier, len(val_peers) + len(cond_peers))
    own = rows_all.at[cond_pos, val_pos]
    for peer in val_peers:
        remote(row_send.at[peer[0]], own, 0, peer)
    own = cols_all.at[cond_pos, val_pos]
    for peer in cond_peers:
        remote(col_send.at[peer[1]], own, 1, peer)
    wait_for(row_send.at[pl.ds(0, n_val - 1)], recv_sems.at[0])
    own = rows_all.at[cond_pos]
    for peer in cond_peers:
        remote(own, own, 2, peer)
    wait_for(col_send.at[pl.ds(0, n_cond - 1)], recv_sems.at[1])
    own = cols_all.at[:, val_pos]
    for peer in val_peers:
        remote(own, own, 3, peer)
    for at, ref in (
        (2, rows_all.at[pl.ds(0, n_cond - 1)]),
        (3, cols_all.at[:, pl.ds(0, n_val - 1)]),
    ):
        wait_for(ref, recv_sems.at[at])
        wait_for(ref, send_sems.at[at])
    wait_for(row_send.at[pl.ds(0, n_val - 1)], send_sems.at[0])
    wait_for(col_send.at[pl.ds(0, n_cond - 1)], send_sems.at[1])


def chi_kernel(row_segs, col_segs, rows_all, cols_all, out_ref, row_wide, right):
    pairs = row_wide.shape[1] // 16
    lanes = cols_all.shape[1]
    width = col_segs * lanes

    @pl.when(pl.program_id(0) == 0)
    def _():
        for at in range(row_wide.shape[0]):
            row_wide[at] = rows_all[:, 128 * at : 128 * (at + 1)].astype(F32)

        def with_cols(col_wide):
            for at in range(lanes // 128):
                col_wide[...] = cols_all[:, 128 * at : 128 * (at + 1)].astype(F32)
                for seg in range(col_segs):
                    real = col_wide[pl.ds(seg, pairs, stride=16), :]
                    imag = col_wide[pl.ds(seg + 8, pairs, stride=16), :]
                    start = seg * lanes + 128 * at
                    here, there = slice(start, start + 128), slice(width + start, width + start + 128)
                    right[:, here] = jnp.concatenate([real, imag], axis=0).astype(BF16)
                    right[:, there] = jnp.concatenate([-imag, real], axis=0).astype(BF16)

        pl.run_scoped(with_cols, pltpu.VMEM((cols_all.shape[0], 128), F32))

    seg = pl.program_id(0)
    tiles = []
    for at in range(row_wide.shape[0]):
        real = row_wide[at, pl.ds(seg, pairs, stride=16), :]
        imag = row_wide[at, pl.ds(seg + 8, pairs, stride=16), :]
        tiles.append(jnp.concatenate([real, imag], axis=0).T.astype(BF16))
    left = jnp.concatenate(tiles, axis=0)
    for part in range(2):
        out_ref[part] = jnp.dot(
            left, right[:, width * part : width * (part + 1)], preferred_element_type=F32
        )


def flat_rows(orbital):
    return orbital.reshape(2, -1, 128).transpose(1, 0, 2).reshape(-1, 128)


def on_device(counts, orb_val, orb_cond, energies, gvec_map):
    n_val, n_cond = counts
    count_g = gvec_map.shape[0]
    reach = reach_of(SIDE, count_g)
    matrices = [jnp.asarray(m) for m in dft_matrices(reach)]
    rows = 2 * SIDE**3 // 128
    quads = (2 * reach + 1 + 3) // 4
    row_block, col_block = count_g // n_val, count_g // n_cond
    row_lanes, col_lanes = max(128, row_block // 8), max(128, col_block // 8)
    row_segs, col_segs = row_block // row_lanes, col_block // col_lanes
    vmem = pl.BlockSpec(memory_space=pltpu.VMEM)
    anywhere = pl.BlockSpec(memory_space=pl.ANY)
    rows_all, cols_all = pl.pallas_call(
        functools.partial(density_kernel, reach, counts),
        out_shape=[
            jax.ShapeDtypeStruct((n_cond, n_val, 16, row_lanes), BF16),
            jax.ShapeDtypeStruct((n_cond, n_val, 16, col_lanes), BF16),
        ],
        in_specs=[anywhere, anywhere, vmem, vmem, anywhere, anywhere, anywhere],
        out_specs=[vmem, vmem],
        scratch_shapes=[
            pltpu.VMEM((rows, 128), BF16),
            pltpu.VMEM((rows, 128), BF16),
            pltpu.VMEM(matrices[0].shape, BF16),
            pltpu.VMEM(matrices[1].shape, BF16),
            pltpu.VMEM(matrices[2].shape, BF16),
            pltpu.VMEM((rows, 128), F32),
            pltpu.VMEM((rows, 128), F32),
            pltpu.VMEM((4, SIDE // 4 * SIDE // 2, 6 * 128), BF16),
            pltpu.VMEM((SIDE * PAD, 128), F32),
            pltpu.VMEM((2 * PAD, 128 * quads), BF16),
            pltpu.VMEM((n_val, 16, row_lanes), F32),
            pltpu.VMEM((n_cond, 16, col_lanes), F32),
            pltpu.VMEM((n_val, 16, row_lanes), BF16),
            pltpu.VMEM((n_cond, 16, col_lanes), BF16),
            pltpu.SemaphoreType.DMA((11,)),
            pltpu.SemaphoreType.DMA((4,)),
            pltpu.SemaphoreType.DMA((4,)),
        ],
        compiler_params=pltpu.CompilerParams(
            vmem_limit_bytes=48 * 2**20, collective_id=0, has_side_effects=True
        ),
        name="density",
    )(flat_rows(orb_val), flat_rows(orb_cond), gvec_map.reshape(1, count_g), energies, *matrices)
    high = n_cond * n_val * 16
    return pl.pallas_call(
        functools.partial(chi_kernel, row_segs, col_segs),
        grid=(row_segs,),
        out_shape=jax.ShapeDtypeStruct((2, row_block, col_block), F32),
        in_specs=[vmem, vmem],
        out_specs=pl.BlockSpec((2, row_lanes, col_block), lambda seg: (0, seg, 0)),
        scratch_shapes=[
            pltpu.VMEM((row_lanes // 128, high, 128), F32),
            pltpu.VMEM((high // 8, 2 * col_block), BF16),
        ],
        compiler_params=pltpu.CompilerParams(vmem_limit_bytes=48 * 2**20),
        name="chi",
    )(rows_all.reshape(high, row_lanes), cols_all.reshape(high, col_lanes))


def solution(mesh):
    return jax.shard_map(
        functools.partial(on_device, (mesh.shape["val"], mesh.shape["cond"])),
        mesh=mesh,
        in_specs=(P(None, "val", None), P(None, "cond", None), P(), P()),
        out_specs=P(None, "val", "cond"),
        check_vma=False,
    )
```

```python
import functools
import math

import jax
import jax.numpy as jnp
import ml_dtypes
import numpy as np
from jax import lax
from jax.experimental import pallas as pl
from jax.experimental.pallas import tpu as pltpu
from jax.sharding import PartitionSpec as P

SIDE = 64
PAD = 32
F32 = jnp.float32
BF16 = jnp.bfloat16
MESH = pl.DeviceIdType.MESH


def reach_of(side, count_g):
    wave = np.arange(side)
    signed = np.where(wave >= side // 2, wave - side, wave)
    squares = signed * signed
    radius = (squares[:, None, None] + squares[None, :, None] + squares[None, None, :]).reshape(-1)
    return math.isqrt(int(np.sort(radius)[count_g - 1]))


def split_high_low(matrix, axis):
    high = matrix.astype(ml_dtypes.bfloat16)
    low = (matrix - high.astype(np.float64)).astype(ml_dtypes.bfloat16)
    return np.concatenate([high, high, low], axis=axis)


def dft_matrices(reach):
    width = 2 * reach + 1
    waves = np.arange(width) - reach
    angle = 2.0 * np.pi * ((waves[None, :] * np.arange(SIDE)[:, None]) % SIDE) / SIDE
    cosine = np.zeros((SIDE, PAD))
    sine = np.zeros((SIDE, PAD))
    cosine[:, :width] = np.cos(angle)
    sine[:, :width] = np.sin(angle)
    full = np.zeros((2, SIDE, 2, PAD))
    full[0, :, 0] = cosine
    full[1, :, 0] = sine
    full[0, :, 1] = -sine
    full[1, :, 1] = cosine
    along_z = np.zeros((2, 2, SIDE, 2, 2, PAD))
    for low in range(2):
        along_z[:, low, :, :, low, :] = full
    along_z = along_z.reshape(4 * SIDE, 4 * PAD)
    along_y = full.reshape(2, SIDE // 2, 2, 2, PAD).transpose(3, 4, 0, 2, 1).reshape(2 * PAD, 2 * SIDE)
    along_x = full.transpose(2, 3, 0, 1).reshape(2 * PAD, 2 * SIDE) * float(SIDE) ** -1.5
    return split_high_low(along_z, 0), split_high_low(along_y, 1), split_high_low(along_x, 1)


def high_low(value):
    high = value.astype(BF16)
    return high, (value - high.astype(F32)).astype(BF16)


def regroup(parts, lane):
    results = []
    for j in range(4):
        total = None
        for i, part in enumerate(parts):
            shift = (32 * (i - j)) % 128
            moved = pltpu.roll(part, shift, 1) if shift else part
            total = moved if total is None else jnp.where(lane == i, moved, total)
        results.append(total)
    return results


def cube_of(
    ready, weights_ready, val_ref, cond_ref, along_z, along_y, along_x, val_wide, cond_wide, by_z, by_y, quads
):
    half = SIDE // 2
    quarter = SIDE // 4
    for x_high in range(quarter):
        rows = 4 * half
        if x_high % 4 == 0:
            ready(x_high // 4)
        both = slice(2 * rows * x_high, 2 * rows * (x_high + 1))
        val_wide[both] = val_ref[both].astype(F32)
        cond_wide[both] = cond_ref[both].astype(F32)
        real_rows = pl.ds(2 * rows * x_high, rows, stride=2)
        imag_rows = pl.ds(2 * rows * x_high + 1, rows, stride=2)
        val_real, val_imag = val_wide[real_rows, :], val_wide[imag_rows, :]
        cond_real, cond_imag = cond_wide[real_rows, :], cond_wide[imag_rows, :]
        real_high, real_low = high_low(val_real * cond_real + val_imag * cond_imag)
        imag_high, imag_low = high_low(val_real * cond_imag - val_imag * cond_real)
        for x_low in range(4):
            here = slice(half * x_low, half * (x_low + 1))
            there = slice(half * x_high, half * (x_high + 1))
            pieces = (real_high, imag_high, real_low, imag_low, real_high, imag_high)
            for at, piece in enumerate(pieces):
                by_z[x_low, there, 128 * at : 128 * (at + 1)] = piece[here]
    weights_ready()
    lane = lax.broadcasted_iota(jnp.int32, (1, 128), 1) // 32
    step = 128
    for start in range(0, quarter * half, step):
        parts = [
            jnp.dot(by_z[x_low, start : start + step, :], along_z[...], preferred_element_type=F32)
            for x_low in range(4)
        ]
        grouped = regroup(parts, lane)
        for inner in range(step // half):
            block = jnp.concatenate([g[half * inner : half * (inner + 1)] for g in grouped], axis=0)
            high, low = high_low(block)
            stacked = jnp.concatenate([high, low, high], axis=0)
            turned = jnp.dot(along_y[...], stacked, preferred_element_type=F32)
            x_high = start // half + inner
            by_y[128 * x_high : 128 * (x_high + 1), :] = jnp.concatenate([turned, turned], axis=0).T
    cubes = []
    for quad in range(quads):
        blocks = [by_y[pl.ds(4 * quad + i, SIDE, stride=PAD), :] for i in range(4)]
        real, imag = regroup(blocks, lane)[:2]
        high, low = high_low(jnp.concatenate([real, imag], axis=0))
        stacked = jnp.concatenate([high, low, high], axis=0)
        cubes.append(jnp.dot(along_x[...], stacked, preferred_element_type=F32).astype(BF16))
    return jnp.concatenate(cubes, axis=1)


def pick(cube, cells, reach):
    count = cells.shape[1]
    x_pos = ((cells >> 12) + reach) & (SIDE - 1)
    y_pos = ((cells >> 6) + reach) & (SIDE - 1)
    z_pos = (cells + reach) & (SIDE - 1)
    place = z_pos * PAD + y_pos
    rows = lax.broadcasted_iota(jnp.int32, (cube.shape[1], count), 0)
    chosen = jnp.where(rows == place, 1.0, 0.0).astype(BF16)
    lines = jnp.dot(cube, chosen, preferred_element_type=F32)
    plane = lax.broadcasted_iota(jnp.int32, (PAD, count), 0) == x_pos
    real = jnp.sum(jnp.where(plane, lines[:PAD], 0.0), axis=0, keepdims=True)
    imag = jnp.sum(jnp.where(plane, lines[PAD:], 0.0), axis=0, keepdims=True)
    return real, imag


def density_kernel(
    reach,
    counts,
    val_ref,
    cond_ref,
    gvec_in,
    energy_in,
    wz_ref,
    wy_ref,
    wx_ref,
    rows_all,
    cols_all,
    val_in,
    cond_in,
    gvec_ref,
    energy_ref,
    along_z,
    along_y,
    along_x,
    val_wide,
    cond_wide,
    by_z,
    by_y,
    cube_ref,
    row_stage,
    col_stage,
    row_send,
    col_send,
    in_sems,
    send_sems,
    recv_sems,
):
    n_val, n_cond = counts
    val_pos = lax.axis_index("val")
    cond_pos = lax.axis_index("cond")
    val_peers = [(lax.rem(val_pos + step, n_val), cond_pos) for step in range(1, n_val)]
    cond_peers = [(val_pos, lax.rem(cond_pos + step, n_cond)) for step in range(1, n_cond)]
    barrier = pltpu.get_barrier_semaphore()
    for peer in val_peers + cond_peers:
        pl.semaphore_signal(barrier, inc=1, device_id=peer, device_id_type=MESH)

    loads = [
        pltpu.make_async_copy(source, target, in_sems.at[at])
        for at, (source, target) in enumerate(
            (
                (wz_ref, along_z),
                (wy_ref, along_y),
                (wx_ref, along_x),
                (gvec_in, gvec_ref),
                (energy_in, energy_ref),
            )
        )
    ]
    chunks = 4
    rows = val_in.shape[0] // chunks
    for chunk in range(chunks):
        here = slice(rows * chunk, rows * (chunk + 1))
        loads.append(pltpu.make_async_copy(val_ref.at[here], val_in.at[here], in_sems.at[5 + 2 * chunk]))
        loads.append(pltpu.make_async_copy(cond_ref.at[here], cond_in.at[here], in_sems.at[6 + 2 * chunk]))
    for load in loads[5:] + loads[:5]:
        load.start()

    def ready(chunk):
        loads[5 + 2 * chunk].wait()
        loads[6 + 2 * chunk].wait()

    def weights_ready():
        for load in loads[:5]:
            load.wait()

    quads = (2 * reach + 1 + 3) // 4
    cube_ref[...] = cube_of(
        ready, weights_ready, val_in, cond_in, along_z, along_y, along_x, val_wide, cond_wide, by_z, by_y, quads
    )
    total = float(energy_ref.shape[0] * energy_ref.shape[1])
    weights = -2.0 / (total * energy_ref[...])
    mine = (lax.broadcasted_iota(jnp.int32, weights.shape, 0) == val_pos) & (
        lax.broadcasted_iota(jnp.int32, weights.shape, 1) == cond_pos
    )
    weight = jnp.sum(jnp.where(mine, weights, 0.0))

    row_lanes, col_lanes = rows_all.shape[3], cols_all.shape[3]
    count_g = gvec_ref.shape[1]
    row_block = count_g // n_val
    row_segs = row_block // row_lanes
    col_segs = count_g // n_cond // col_lanes
    ratio = n_cond // n_val
    step = min(512, row_block)
    if row_segs < 8:
        row_stage[...] = jnp.zeros_like(row_stage)
    if col_segs < 8:
        col_stage[...] = jnp.zeros_like(col_stage)

    def gather(block):
        @pl.loop(0, row_block // step)
        def _(at):
            start = block * row_block + at * step
            picked = pick(cube_ref[...], gvec_ref[:, pl.ds(pl.multiple_of(start, step), step)], reach)
            for stage, lanes, segs in ((row_stage, row_lanes, row_segs), (col_stage, col_lanes, col_segs)):
                for piece in range(step // lanes):
                    whole = at * (step // lanes) + piece
                    for part in range(2):
                        stage[whole // segs, pl.ds(whole % segs + 8 * part, 1), :] = picked[part][
                            :, lanes * piece : lanes * (piece + 1)
                        ]

    def remote(source, target, sems, peer):
        pltpu.make_async_remote_copy(
            src_ref=source,
            dst_ref=target,
            send_sem=sems[0],
            recv_sem=sems[1],
            device_id=peer,
            device_id_type=MESH,
        ).start()

    def wait_for(ref, sem):
        pltpu.make_async_copy(ref, ref, sem).wait()

    col_sems = (send_sems.at[0], recv_sems.at[0])
    col_late = (send_sems.at[1], recv_sems.at[1])
    row_late = (send_sems.at[2], recv_sems.at[2])

    def spread(val_from):
        piece = rows_all.at[cond_pos, val_from]
        for peer in cond_peers:
            remote(piece, piece, row_late, peer)

    def arrived(distance):
        wait_for(row_send.at[0], recv_sems.at[3 + distance])
        spread(lax.rem(val_pos + n_val - distance, n_val))

    for distance in range(n_val):
        block = lax.rem(val_pos + distance, n_val)
        gather(block)
        if distance == 0:
            pl.semaphore_wait(barrier, len(val_peers) + len(cond_peers))
        ready_rows = (weight * row_stage[0].astype(BF16).astype(F32)).astype(BF16)
        if distance == 0:
            rows_all[cond_pos, val_pos] = ready_rows
            spread(val_pos)
        else:
            row_send[distance - 1] = ready_rows
            own = rows_all.at[cond_pos, val_pos]
            sems = (send_sems.at[3 + distance], recv_sems.at[3 + distance])
            remote(row_send.at[distance - 1], own, sems, (block, cond_pos))
        for at in range(ratio):
            target = block * ratio + at
            col_send[target] = col_stage[at].astype(BF16)

            @pl.when(target != cond_pos)
            def _():
                own = cols_all.at[cond_pos, val_pos]
                remote(col_send.at[target], own, col_sems, (val_pos, target))

        if distance > 1:
            arrived(distance - 1)
    cols_all[cond_pos, val_pos] = col_send[cond_pos]
    if n_val > 1:
        arrived(n_val - 1)
    wait_for(col_send.at[pl.ds(0, n_cond - 1)], col_sems[1])
    own = cols_all.at[:, val_pos]
    for peer in val_peers:
        remote(own, own, col_late, peer)
    for ref, sems in (
        (rows_all.at[pl.ds(0, n_cond - 1)], row_late),
        (cols_all.at[:, pl.ds(0, n_val - 1)], col_late),
    ):
        wait_for(ref, sems[1])
        wait_for(ref, sems[0])
    for distance in range(1, n_val):
        wait_for(row_send.at[0], send_sems.at[3 + distance])
    wait_for(col_send.at[pl.ds(0, n_cond - 1)], col_sems[0])


def chi_kernel(row_segs, col_segs, rows_all, cols_all, out_ref, row_wide, right):
    pairs = row_wide.shape[1] // 16
    lanes = cols_all.shape[1]
    width = col_segs * lanes

    @pl.when(pl.program_id(0) == 0)
    def _():
        for at in range(row_wide.shape[0]):
            row_wide[at] = rows_all[:, 128 * at : 128 * (at + 1)].astype(F32)

        def with_cols(col_wide):
            for at in range(lanes // 128):
                col_wide[...] = cols_all[:, 128 * at : 128 * (at + 1)].astype(F32)
                for seg in range(col_segs):
                    real = col_wide[pl.ds(seg, pairs, stride=16), :]
                    imag = col_wide[pl.ds(seg + 8, pairs, stride=16), :]
                    start = seg * lanes + 128 * at
                    here, there = slice(start, start + 128), slice(width + start, width + start + 128)
                    right[:, here] = jnp.concatenate([real, imag], axis=0).astype(BF16)
                    right[:, there] = jnp.concatenate([-imag, real], axis=0).astype(BF16)

        pl.run_scoped(with_cols, pltpu.VMEM((cols_all.shape[0], 128), F32))

    seg = pl.program_id(0)
    tiles = []
    for at in range(row_wide.shape[0]):
        real = row_wide[at, pl.ds(seg, pairs, stride=16), :]
        imag = row_wide[at, pl.ds(seg + 8, pairs, stride=16), :]
        tiles.append(jnp.concatenate([real, imag], axis=0).T.astype(BF16))
    left = jnp.concatenate(tiles, axis=0)
    for part in range(2):
        out_ref[part] = jnp.dot(
            left, right[:, width * part : width * (part + 1)], preferred_element_type=F32
        )


def flat_rows(orbital):
    return orbital.reshape(2, -1, 128).transpose(1, 0, 2).reshape(-1, 128)


def on_device(counts, orb_val, orb_cond, energies, gvec_map):
    n_val, n_cond = counts
    count_g = gvec_map.shape[0]
    reach = reach_of(SIDE, count_g)
    matrices = [jnp.asarray(m) for m in dft_matrices(reach)]
    rows = 2 * SIDE**3 // 128
    quads = (2 * reach + 1 + 3) // 4
    row_block, col_block = count_g // n_val, count_g // n_cond
    row_lanes, col_lanes = max(128, row_block // 8), max(128, col_block // 8)
    row_segs, col_segs = row_block // row_lanes, col_block // col_lanes
    vmem = pl.BlockSpec(memory_space=pltpu.VMEM)
    hbm = pl.BlockSpec(memory_space=pltpu.HBM)
    rows_all, cols_all = pl.pallas_call(
        functools.partial(density_kernel, reach, counts),
        out_shape=[
            jax.ShapeDtypeStruct((n_cond, n_val, 16, row_lanes), BF16),
            jax.ShapeDtypeStruct((n_cond, n_val, 16, col_lanes), BF16),
        ],
        in_specs=[hbm] * 7,
        out_specs=[vmem, vmem],
        scratch_shapes=[
            pltpu.VMEM((rows, 128), BF16),
            pltpu.VMEM((rows, 128), BF16),
            pltpu.VMEM((1, count_g), jnp.int32),
            pltpu.VMEM(energies.shape, F32),
            pltpu.VMEM(matrices[0].shape, BF16),
            pltpu.VMEM(matrices[1].shape, BF16),
            pltpu.VMEM(matrices[2].shape, BF16),
            pltpu.VMEM((rows, 128), F32),
            pltpu.VMEM((rows, 128), F32),
            pltpu.VMEM((4, SIDE // 4 * SIDE // 2, 6 * 128), BF16),
            pltpu.VMEM((SIDE * PAD, 128), F32),
            pltpu.VMEM((2 * PAD, 128 * quads), BF16),
            pltpu.VMEM((1, 16, row_lanes), F32),
            pltpu.VMEM((n_cond // n_val, 16, col_lanes), F32),
            pltpu.VMEM((n_val, 16, row_lanes), BF16),
            pltpu.VMEM((n_cond, 16, col_lanes), BF16),
            pltpu.SemaphoreType.DMA((13,)),
            pltpu.SemaphoreType.DMA((3 + n_val,)),
            pltpu.SemaphoreType.DMA((3 + n_val,)),
        ],
        compiler_params=pltpu.CompilerParams(
            vmem_limit_bytes=62 * 2**20, collective_id=0, has_side_effects=True
        ),
        name="density",
    )(flat_rows(orb_val), flat_rows(orb_cond), gvec_map.reshape(1, count_g), energies, *matrices)
    high = n_cond * n_val * 16
    return pl.pallas_call(
        functools.partial(chi_kernel, row_segs, col_segs),
        grid=(row_segs,),
        out_shape=jax.ShapeDtypeStruct((2, row_block, col_block), F32),
        in_specs=[vmem, vmem],
        out_specs=pl.BlockSpec((2, row_lanes, col_block), lambda seg: (0, seg, 0)),
        scratch_shapes=[
            pltpu.VMEM((row_lanes // 128, high, 128), F32),
            pltpu.VMEM((high // 8, 2 * col_block), BF16),
        ],
        compiler_params=pltpu.CompilerParams(vmem_limit_bytes=48 * 2**20),
        name="chi",
    )(rows_all.reshape(high, row_lanes), cols_all.reshape(high, col_lanes))


def solution(mesh):
    return jax.shard_map(
        functools.partial(on_device, (mesh.shape["val"], mesh.shape["cond"])),
        mesh=mesh,
        in_specs=(P(None, "val", None), P(None, "cond", None), P(), P()),
        out_specs=P(None, "val", "cond"),
        check_vma=False,
    )
```

```python
import functools
import math

import jax
import jax.numpy as jnp
import ml_dtypes
import numpy as np
from jax import lax
from jax.experimental import pallas as pl
from jax.experimental.pallas import tpu as pltpu
from jax.sharding import PartitionSpec as P

SIDE = 64
PAD = 32
F32 = jnp.float32
BF16 = jnp.bfloat16
MESH = pl.DeviceIdType.MESH


def reach_of(side, count_g):
    wave = np.arange(side)
    signed = np.where(wave >= side // 2, wave - side, wave)
    squares = signed * signed
    radius = (squares[:, None, None] + squares[None, :, None] + squares[None, None, :]).reshape(-1)
    return math.isqrt(int(np.sort(radius)[count_g - 1]))


def split_high_low(matrix, axis):
    high = matrix.astype(ml_dtypes.bfloat16)
    low = (matrix - high.astype(np.float64)).astype(ml_dtypes.bfloat16)
    return np.concatenate([high, high, low], axis=axis)


def dft_matrices(reach):
    width = 2 * reach + 1
    waves = np.arange(width) - reach
    angle = 2.0 * np.pi * ((waves[None, :] * np.arange(SIDE)[:, None]) % SIDE) / SIDE
    cosine = np.zeros((SIDE, PAD))
    sine = np.zeros((SIDE, PAD))
    cosine[:, :width] = np.cos(angle)
    sine[:, :width] = np.sin(angle)
    full = np.zeros((2, SIDE, 2, PAD))
    full[0, :, 0] = cosine
    full[1, :, 0] = sine
    full[0, :, 1] = -sine
    full[1, :, 1] = cosine
    along_z = np.zeros((2, 2, SIDE, 2, 2, PAD))
    for low in range(2):
        along_z[:, low, :, :, low, :] = full
    along_z = along_z.reshape(4 * SIDE, 4 * PAD)
    along_y = full.reshape(2, SIDE // 2, 2, 2, PAD).transpose(3, 4, 0, 2, 1).reshape(2 * PAD, 2 * SIDE)
    along_x = full.transpose(2, 3, 0, 1).reshape(2 * PAD, 2 * SIDE) * float(SIDE) ** -1.5
    return split_high_low(along_z, 0), split_high_low(along_y, 1), split_high_low(along_x, 1)


def high_low(value):
    high = value.astype(BF16)
    return high, (value - high.astype(F32)).astype(BF16)


def regroup(parts, lane):
    results = []
    for j in range(4):
        total = None
        for i, part in enumerate(parts):
            shift = (32 * (i - j)) % 128
            moved = pltpu.roll(part, shift, 1) if shift else part
            total = moved if total is None else jnp.where(lane == i, moved, total)
        results.append(total)
    return results


def cube_of(
    ready, weights_ready, val_ref, cond_ref, along_z, along_y, along_x, val_wide, cond_wide, by_z, by_y, quads
):
    half = SIDE // 2
    quarter = SIDE // 4
    for x_high in range(quarter):
        rows = 4 * half
        if x_high % 4 == 0:
            ready(x_high // 4)
        both = slice(2 * rows * x_high, 2 * rows * (x_high + 1))
        val_wide[both] = val_ref[both].astype(F32)
        cond_wide[both] = cond_ref[both].astype(F32)
        real_rows = pl.ds(2 * rows * x_high, rows, stride=2)
        imag_rows = pl.ds(2 * rows * x_high + 1, rows, stride=2)
        val_real, val_imag = val_wide[real_rows, :], val_wide[imag_rows, :]
        cond_real, cond_imag = cond_wide[real_rows, :], cond_wide[imag_rows, :]
        real_high, real_low = high_low(val_real * cond_real + val_imag * cond_imag)
        imag_high, imag_low = high_low(val_real * cond_imag - val_imag * cond_real)
        for x_low in range(4):
            here = slice(half * x_low, half * (x_low + 1))
            there = slice(half * x_high, half * (x_high + 1))
            pieces = (real_high, imag_high, real_low, imag_low, real_high, imag_high)
            for at, piece in enumerate(pieces):
                by_z[x_low, there, 128 * at : 128 * (at + 1)] = piece[here]
    weights_ready()
    lane = lax.broadcasted_iota(jnp.int32, (1, 128), 1) // 32
    step = 128
    for start in range(0, quarter * half, step):
        parts = [
            jnp.dot(by_z[x_low, start : start + step, :], along_z[...], preferred_element_type=F32)
            for x_low in range(4)
        ]
        grouped = regroup(parts, lane)
        for inner in range(step // half):
            block = jnp.concatenate([g[half * inner : half * (inner + 1)] for g in grouped], axis=0)
            high, low = high_low(block)
            stacked = jnp.concatenate([high, low, high], axis=0)
            turned = jnp.dot(along_y[...], stacked, preferred_element_type=F32)
            x_high = start // half + inner
            by_y[128 * x_high : 128 * (x_high + 1), :] = jnp.concatenate([turned, turned], axis=0).T
    cubes = []
    for quad in range(quads):
        blocks = [by_y[pl.ds(4 * quad + i, SIDE, stride=PAD), :] for i in range(4)]
        real, imag = regroup(blocks, lane)[:2]
        high, low = high_low(jnp.concatenate([real, imag], axis=0))
        stacked = jnp.concatenate([high, low, high], axis=0)
        cubes.append(jnp.dot(along_x[...], stacked, preferred_element_type=F32).astype(BF16))
    return jnp.concatenate(cubes, axis=1)


def pick(cube, cells, reach):
    count = cells.shape[1]
    x_pos = ((cells >> 12) + reach) & (SIDE - 1)
    y_pos = ((cells >> 6) + reach) & (SIDE - 1)
    z_pos = (cells + reach) & (SIDE - 1)
    place = z_pos * PAD + y_pos
    rows = lax.broadcasted_iota(jnp.int32, (cube.shape[1], count), 0)
    hit = rows.astype(jnp.int16) == place.astype(jnp.int16)
    chosen = jnp.where(hit, jnp.ones((), BF16), jnp.zeros((), BF16))
    lines = jnp.dot(cube, chosen, preferred_element_type=F32)
    plane = lax.broadcasted_iota(jnp.int32, (PAD, count), 0) == x_pos
    real = jnp.sum(jnp.where(plane, lines[:PAD], 0.0), axis=0, keepdims=True)
    imag = jnp.sum(jnp.where(plane, lines[PAD:], 0.0), axis=0, keepdims=True)
    return real, imag


def density_kernel(
    reach,
    counts,
    val_ref,
    cond_ref,
    gvec_in,
    energy_in,
    wz_ref,
    wy_ref,
    wx_ref,
    rows_all,
    cols_all,
    val_in,
    cond_in,
    gvec_ref,
    energy_ref,
    along_z,
    along_y,
    along_x,
    val_wide,
    cond_wide,
    by_z,
    by_y,
    cube_ref,
    row_stage,
    col_stage,
    row_send,
    col_send,
    in_sems,
    send_sems,
    recv_sems,
    far_sems,
):
    n_val, n_cond = counts
    val_pos = lax.axis_index("val")
    cond_pos = lax.axis_index("cond")
    val_peers = [(lax.rem(val_pos + step, n_val), cond_pos) for step in range(1, n_val)]
    cond_peers = [(val_pos, lax.rem(cond_pos + step, n_cond)) for step in range(1, n_cond)]
    barrier = pltpu.get_barrier_semaphore()
    for peer in val_peers + cond_peers:
        pl.semaphore_signal(barrier, inc=1, device_id=peer, device_id_type=MESH)

    loads = [
        pltpu.make_async_copy(source, target, in_sems.at[at])
        for at, (source, target) in enumerate(
            (
                (wz_ref, along_z),
                (wy_ref, along_y),
                (wx_ref, along_x),
                (gvec_in, gvec_ref),
                (energy_in, energy_ref),
            )
        )
    ]
    chunks = 4
    rows = val_in.shape[0] // chunks
    for chunk in range(chunks):
        here = slice(rows * chunk, rows * (chunk + 1))
        loads.append(pltpu.make_async_copy(val_ref.at[here], val_in.at[here], in_sems.at[5 + 2 * chunk]))
        loads.append(pltpu.make_async_copy(cond_ref.at[here], cond_in.at[here], in_sems.at[6 + 2 * chunk]))
    for load in loads[5:] + loads[:5]:
        load.start()

    def ready(chunk):
        loads[5 + 2 * chunk].wait()
        loads[6 + 2 * chunk].wait()

    def weights_ready():
        for load in loads[:5]:
            load.wait()

    quads = (2 * reach + 1 + 3) // 4
    cube_ref[...] = cube_of(
        ready, weights_ready, val_in, cond_in, along_z, along_y, along_x, val_wide, cond_wide, by_z, by_y, quads
    )
    total = float(energy_ref.shape[0] * energy_ref.shape[1])
    weights = -2.0 / (total * energy_ref[...])
    mine = (lax.broadcasted_iota(jnp.int32, weights.shape, 0) == val_pos) & (
        lax.broadcasted_iota(jnp.int32, weights.shape, 1) == cond_pos
    )
    weight = jnp.sum(jnp.where(mine, weights, 0.0))

    row_lanes, col_lanes = rows_all.shape[3], cols_all.shape[3]
    count_g = gvec_ref.shape[1]
    row_block = count_g // n_val
    row_segs = row_block // row_lanes
    col_segs = count_g // n_cond // col_lanes
    ratio = n_cond // n_val
    step = min(512, row_block)
    if row_segs < 8:
        row_stage[...] = jnp.zeros_like(row_stage)
    if col_segs < 8:
        col_stage[...] = jnp.zeros_like(col_stage)

    def gather(block):
        @pl.loop(0, row_block // step)
        def _(at):
            start = block * row_block + at * step
            picked = pick(cube_ref[...], gvec_ref[:, pl.ds(pl.multiple_of(start, step), step)], reach)
            for stage, lanes, segs in ((row_stage, row_lanes, row_segs), (col_stage, col_lanes, col_segs)):
                for piece in range(step // lanes):
                    whole = at * (step // lanes) + piece
                    for part in range(2):
                        stage[whole // segs, pl.ds(whole % segs + 8 * part, 1), :] = picked[part][
                            :, lanes * piece : lanes * (piece + 1)
                        ]

    def remote(source, target, sems, peer):
        pltpu.make_async_remote_copy(
            src_ref=source,
            dst_ref=target,
            send_sem=sems[0],
            recv_sem=sems[1],
            device_id=peer,
            device_id_type=MESH,
        ).start()

    def wait_for(ref, sem):
        pltpu.make_async_copy(ref, ref, sem).wait()

    col_sems = (send_sems.at[0], recv_sems.at[0])
    col_late = (send_sems.at[1], recv_sems.at[1])
    row_late = (send_sems.at[2], recv_sems.at[2])

    n_far = n_cond // 2
    far, near = cond_pos // 2, lax.rem(cond_pos, 2)
    partner = (val_pos, far * 2 + 1 - near)

    def source_of(distance):
        return lax.rem(val_pos + n_val - distance, n_val)

    def spread(distance):
        piece = rows_all.at[cond_pos, source_of(distance)]
        for hop in range(1, n_far):
            peer = (val_pos, lax.rem(far + hop, n_far) * 2 + near)
            remote(piece, piece, (send_sems.at[2], far_sems.at[hop, distance]), peer)
        remote(piece, piece, row_late, partner)

    def arrived(distance):
        wait_for(row_send.at[0], recv_sems.at[3 + distance])
        spread(distance)

    def forward(distance):
        for hop in range(1, n_far):
            wait_for(row_send.at[0], far_sems.at[hop, distance])
            origin = lax.rem(far + n_far - hop, n_far) * 2 + near
            piece = rows_all.at[origin, source_of(distance)]
            remote(piece, piece, row_late, partner)

    for distance in range(n_val):
        block = lax.rem(val_pos + distance, n_val)
        gather(block)
        if distance == 0:
            pl.semaphore_wait(barrier, len(val_peers) + len(cond_peers))
        ready_rows = (weight * row_stage[0].astype(BF16).astype(F32)).astype(BF16)
        if distance == 0:
            rows_all[cond_pos, val_pos] = ready_rows
            spread(0)
        else:
            row_send[distance - 1] = ready_rows
            own = rows_all.at[cond_pos, val_pos]
            sems = (send_sems.at[3 + distance], recv_sems.at[3 + distance])
            remote(row_send.at[distance - 1], own, sems, (block, cond_pos))
        for at in range(ratio):
            target = block * ratio + at
            col_send[target] = col_stage[at].astype(BF16)

            @pl.when(target != cond_pos)
            def _():
                own = cols_all.at[cond_pos, val_pos]
                remote(col_send.at[target], own, col_sems, (val_pos, target))

        if distance > 1:
            arrived(distance - 1)
        if distance == 1:
            forward(0)
        if distance > 2:
            forward(distance - 2)
    cols_all[cond_pos, val_pos] = col_send[cond_pos]
    if n_val > 1:
        arrived(n_val - 1)
    wait_for(col_send.at[pl.ds(0, n_cond - 1)], col_sems[1])
    own = cols_all.at[:, val_pos]
    for peer in val_peers:
        remote(own, own, col_late, peer)
    if n_val > 2:
        forward(n_val - 2)
    if n_val > 1:
        forward(n_val - 1)
    wait_for(rows_all.at[pl.ds(0, n_far)], row_late[1])
    wait_for(rows_all.at[pl.ds(0, n_cond - 1)], row_late[0])
    late = cols_all.at[:, pl.ds(0, n_val - 1)]
    wait_for(late, col_late[1])
    wait_for(late, col_late[0])
    for distance in range(1, n_val):
        wait_for(row_send.at[0], send_sems.at[3 + distance])
    wait_for(col_send.at[pl.ds(0, n_cond - 1)], col_sems[0])


def chi_kernel(col_segs, rows_hbm, cols_hbm, out_ref, rows_all, cols_all, row_wide, right, sems):
    pairs = row_wide.shape[1] // 16
    lanes = cols_all.shape[1]
    width = col_segs * lanes

    @pl.when(pl.program_id(0) == 0)
    def _():
        cols_load = pltpu.make_async_copy(cols_hbm, cols_all, sems.at[0])
        rows_load = pltpu.make_async_copy(rows_hbm, rows_all, sems.at[1])
        cols_load.start()
        rows_load.start()
        cols_load.wait()

        def with_cols(col_wide):
            for at in range(lanes // 128):
                col_wide[...] = cols_all[:, 128 * at : 128 * (at + 1)].astype(F32)
                for seg in range(col_segs):
                    real = col_wide[pl.ds(seg, pairs, stride=16), :]
                    imag = col_wide[pl.ds(seg + 8, pairs, stride=16), :]
                    start = seg * lanes + 128 * at
                    here, there = slice(start, start + 128), slice(width + start, width + start + 128)
                    right[:, here] = jnp.concatenate([real, imag], axis=0).astype(BF16)
                    right[:, there] = jnp.concatenate([-imag, real], axis=0).astype(BF16)

        pl.run_scoped(with_cols, pltpu.VMEM((cols_all.shape[0], 128), F32))
        rows_load.wait()
        for at in range(row_wide.shape[0]):
            row_wide[at] = rows_all[:, 128 * at : 128 * (at + 1)].astype(F32)

    seg = pl.program_id(0)
    tiles = []
    for at in range(row_wide.shape[0]):
        real = row_wide[at, pl.ds(seg, pairs, stride=16), :]
        imag = row_wide[at, pl.ds(seg + 8, pairs, stride=16), :]
        tiles.append(jnp.concatenate([real, imag], axis=0).T.astype(BF16))
    left = jnp.concatenate(tiles, axis=0)
    for part in range(2):
        out_ref[part] = jnp.dot(
            left, right[:, width * part : width * (part + 1)], preferred_element_type=F32
        )


def flat_rows(orbital):
    return orbital.reshape(2, -1, 128).transpose(1, 0, 2).reshape(-1, 128)


def on_device(counts, orb_val, orb_cond, energies, gvec_map):
    n_val, n_cond = counts
    count_g = gvec_map.shape[0]
    reach = reach_of(SIDE, count_g)
    matrices = [jnp.asarray(m) for m in dft_matrices(reach)]
    rows = 2 * SIDE**3 // 128
    quads = (2 * reach + 1 + 3) // 4
    row_block, col_block = count_g // n_val, count_g // n_cond
    row_lanes, col_lanes = max(128, row_block // 8), max(128, col_block // 8)
    row_segs, col_segs = row_block // row_lanes, col_block // col_lanes
    vmem = pl.BlockSpec(memory_space=pltpu.VMEM)
    hbm = pl.BlockSpec(memory_space=pltpu.HBM)
    rows_all, cols_all = pl.pallas_call(
        functools.partial(density_kernel, reach, counts),
        out_shape=[
            jax.ShapeDtypeStruct((n_cond, n_val, 16, row_lanes), BF16),
            jax.ShapeDtypeStruct((n_cond, n_val, 16, col_lanes), BF16),
        ],
        in_specs=[hbm] * 7,
        out_specs=[vmem, vmem],
        scratch_shapes=[
            pltpu.VMEM((rows, 128), BF16),
            pltpu.VMEM((rows, 128), BF16),
            pltpu.VMEM((1, count_g), jnp.int32),
            pltpu.VMEM(energies.shape, F32),
            pltpu.VMEM(matrices[0].shape, BF16),
            pltpu.VMEM(matrices[1].shape, BF16),
            pltpu.VMEM(matrices[2].shape, BF16),
            pltpu.VMEM((rows, 128), F32),
            pltpu.VMEM((rows, 128), F32),
            pltpu.VMEM((4, SIDE // 4 * SIDE // 2, 6 * 128), BF16),
            pltpu.VMEM((SIDE * PAD, 128), F32),
            pltpu.VMEM((2 * PAD, 128 * quads), BF16),
            pltpu.VMEM((1, 16, row_lanes), F32),
            pltpu.VMEM((n_cond // n_val, 16, col_lanes), F32),
            pltpu.VMEM((n_val, 16, row_lanes), BF16),
            pltpu.VMEM((n_cond, 16, col_lanes), BF16),
            pltpu.SemaphoreType.DMA((13,)),
            pltpu.SemaphoreType.DMA((3 + n_val,)),
            pltpu.SemaphoreType.DMA((3 + n_val,)),
            pltpu.SemaphoreType.DMA((n_cond // 2, n_val)),
        ],
        compiler_params=pltpu.CompilerParams(
            vmem_limit_bytes=62 * 2**20, collective_id=0, has_side_effects=True
        ),
        name="density",
    )(flat_rows(orb_val), flat_rows(orb_cond), gvec_map.reshape(1, count_g), energies, *matrices)
    high = n_cond * n_val * 16
    return pl.pallas_call(
        functools.partial(chi_kernel, col_segs),
        grid=(row_segs,),
        out_shape=jax.ShapeDtypeStruct((2, row_block, col_block), F32),
        in_specs=[hbm, hbm],
        out_specs=pl.BlockSpec((2, row_lanes, col_block), lambda seg: (0, seg, 0)),
        scratch_shapes=[
            pltpu.VMEM((high, row_lanes), BF16),
            pltpu.VMEM((high, col_lanes), BF16),
            pltpu.VMEM((row_lanes // 128, high, 128), F32),
            pltpu.VMEM((high // 8, 2 * col_block), BF16),
            pltpu.SemaphoreType.DMA((2,)),
        ],
        compiler_params=pltpu.CompilerParams(vmem_limit_bytes=62 * 2**20),
        name="chi",
    )(rows_all.reshape(high, row_lanes), cols_all.reshape(high, col_lanes))


def solution(mesh):
    return jax.shard_map(
        functools.partial(on_device, (mesh.shape["val"], mesh.shape["cond"])),
        mesh=mesh,
        in_specs=(P(None, "val", None), P(None, "cond", None), P(), P()),
        out_specs=P(None, "val", "cond"),
        check_vma=False,
    )
```
